32 devices in a mesh: groups: 2 (over y), row: 4 (over z), col: 2 (over x), sub: 2 (over core).
Axes of the slice: x: 2, y: 2, z: 4, core: 2. Of those that a mesh axis runs over, the one named last changes fastest.
Arguments:
- normed: bfloat16 [1536, 8192], P(('groups', 'col', 'sub'), 'row'), parts along dimension 0, may hold values from -6 to 6
- queries: bfloat16 [1536, 8192], P(('groups', 'row'), ('col', 'sub')), parts along dimension 0, may hold values from -6 to 6
- stored_keys: bfloat16 [1536, 1024], P('groups', ('col', 'sub')), parts along dimension 0, may hold values from -6 to 6
- stored_values: bfloat16 [1536, 1024], P('groups', ('col', 'sub')), parts along dimension 0, may hold values from -6 to 6
- upstream: bfloat16 [1536, 8192], P(('groups', 'col', 'sub'), 'row'), parts along dimension 0, may hold values from -6 to 6
- query_weight: bfloat16 [16384, 8192], P(('groups', 'row'), ('col', 'sub')), parts along dimension 0, may hold values from -0.0625 to 0.0625
- key_matrix: bfloat16 [16384, 1024], P(('groups', 'row'), ('col', 'sub')), parts along dimension 0, may hold values from -0.0625 to 0.0625
- value_matrix: bfloat16 [16384, 1024], P(('groups', 'row'), ('col', 'sub')), parts along dimension 0, may hold values from -0.0625 to 0.0625
- output_weight: bfloat16 [16384, 8192], P(('groups', 'col', 'sub'), 'row'), parts along dimension 0, may hold values from -0.0625 to 0.0625
Outputs:
- grad_normed: bfloat16 [1536, 8192], P(('groups', 'col', 'sub'), 'row'), parts along dimension 0
- grad_query: bfloat16 [16384, 8192], P(('groups', 'row'), ('col', 'sub')), parts along dimension 0
- grad_key: bfloat16 [16384, 1024], P(('groups', 'row'), ('col', 'sub')), parts along dimension 0
- grad_value: bfloat16 [16384, 1024], P(('groups', 'row'), ('col', 'sub')), parts along dimension 0
- grad_output: bfloat16 [16384, 8192], P(('groups', 'col', 'sub'), 'row'), parts along dimension 0
The draws below stay inside these ranges and needn't reach their ends.
There are 2 independent parts, one for each index of `groups`. The reference program is written for one: setup_inputs(seed, part) draws one part's arguments, and reference() takes and returns one part's arrays. A program takes and returns all parts, laid end to end along the dimension named above; each array names one. Nothing has to cross between parts.
All inputs are finite; a program needn't handle non-finite values.
Results may differ from the reference program's by a relative error of at most 0.022.
Values may be sent and summed in bfloat16 or wider, within the bound.
No kernel may reach another device: no remote copies, remote signals or barrier semaphores. Data moves between devices by JAX's collectives and lax.ppermute only.
A program may use at most 128 MiB of HBM per device.

```python
import jax
import jax.numpy as jnp
from jax import lax

MODEL_WIDTH = 8192
QUERY_HEADS = 64
KEY_VALUE_HEADS = 8
HEAD_SIZE = 128
SEQUENCE_LENGTH = 256
SEQUENCE_COUNT = 3
TOKEN_TOTAL = 768
N_ROW = 4


def draw_queries(key, part):
    own_key = jax.random.fold_in(key, 21)
    complete_shape = (TOKEN_TOTAL, QUERY_HEADS * HEAD_SIZE)
    sampled_values = jnp.clip(jax.random.normal(own_key, complete_shape, jnp.float32), -4.0, 4.0)
    return sampled_values.astype(jnp.bfloat16)


def draw_stored_keys(key, part):
    own_key = jax.random.fold_in(key, 22)
    complete_shape = (TOKEN_TOTAL, KEY_VALUE_HEADS * HEAD_SIZE)
    sampled_values = jnp.clip(jax.random.normal(own_key, complete_shape, jnp.float32), -4.0, 4.0)
    return sampled_values.astype(jnp.bfloat16)


def with_spikes(array, key, source, target, shards_of, factor):
    def block_of(position):
        return (jnp.arange(array.shape[position]) // (array.shape[position] // shards_of)).reshape((-1,) + (1,) * (array.ndim - 1 - position))

    near = jax.random.permutation(key, shards_of)[block_of(target)]
    other_side = (block_of(target) + shards_of // 2) % shards_of
    return jnp.where((block_of(source) == near) | (block_of(source) == other_side), factor * array, array)


def levels(key, extent, shards, low, largest):
    factor_of = 1.0
    for position, parts in shards:
        draws = jax.random.uniform(jax.random.fold_in(jax.random.fold_in(key, 6), position), (parts,), jnp.float32, low / len(shards), largest / len(shards))
        factor_of = factor_of * jnp.repeat(jnp.exp(draws), extent[position] // parts).reshape((-1,) + (1,) * (len(extent) - 1 - position))
    return factor_of


def gaussian(rng, dims, spread, most, shards=(), kind=jnp.bfloat16):
    factor_of = levels(rng, dims, shards, -0.22, 0.18) if shards else 1.0
    result = jax.random.normal(rng, dims, jnp.float32) * spread * factor_of
    return jnp.minimum(jnp.maximum(result, -most), most).astype(kind)


def gaussian_with(stream_key, extent, scale, most, pieces, heavy, held_as=jnp.bfloat16):
    entries = scale * jax.random.normal(stream_key, extent, jnp.float32)
    if pieces:
        entries = entries * levels(stream_key, extent, pieces, -0.22, 0.18)
    return jnp.clip(with_spikes(entries, jax.random.fold_in(stream_key, 3), *heavy), -most, most).astype(held_as)


def setup_inputs(seed: int = 0, part: int = 0) -> dict:
    arg_keys = jax.random.split(jax.random.key(seed), 10)
    own_keys = jax.random.split(jax.random.fold_in(arg_keys[9], part), 10)
    normed = gaussian(own_keys[0], (TOKEN_TOTAL, MODEL_WIDTH), 1.0, 6.0, ((0, 4), (1, 4)))
    queries = draw_queries(jax.random.fold_in(jax.random.fold_in(arg_keys[9], part), 71), part)
    stored_keys = draw_stored_keys(jax.random.fold_in(jax.random.fold_in(arg_keys[9], part), 71), part)
    stored_values = gaussian(own_keys[3], (TOKEN_TOTAL, KEY_VALUE_HEADS * HEAD_SIZE), 1.0, 6.0, ((1, 4),))
    upstream = gaussian_with(own_keys[4], (TOKEN_TOTAL, MODEL_WIDTH), 1.0, 6.0, ((0, 4), (1, 4)), (1, 0, 4, 2.0))
    query_weight = gaussian(own_keys[5], (MODEL_WIDTH, QUERY_HEADS * HEAD_SIZE), MODEL_WIDTH ** -0.5, 0.0625, ((0, 4), (1, 4)))
    key_matrix = gaussian(own_keys[6], (MODEL_WIDTH, KEY_VALUE_HEADS * HEAD_SIZE), MODEL_WIDTH ** -0.5, 0.0625, ((0, 4), (1, 4)))
    value_matrix = gaussian(own_keys[7], (MODEL_WIDTH, KEY_VALUE_HEADS * HEAD_SIZE), MODEL_WIDTH ** -0.5, 0.0625, ((0, 4), (1, 4)))
    output_weight = gaussian(own_keys[8], (QUERY_HEADS * HEAD_SIZE, MODEL_WIDTH), (QUERY_HEADS * HEAD_SIZE) ** -0.5, 0.0625, ((0, 4), (1, 4)))
    return dict(normed=normed, queries=queries, stored_keys=stored_keys, stored_values=stored_values, upstream=upstream, query_weight=query_weight, key_matrix=key_matrix, value_matrix=value_matrix, output_weight=output_weight)


def one_sequence(blocks):
    query_token_rows, key_token_rows, value_token_rows, gradient_rows = blocks
    group_width = QUERY_HEADS // KEY_VALUE_HEADS
    score_scale = HEAD_SIZE ** -0.5
    query_head_rows = query_token_rows.astype(jnp.float32).reshape(SEQUENCE_LENGTH, KEY_VALUE_HEADS, group_width, HEAD_SIZE)
    gradient_heads = gradient_rows.astype(jnp.float32).reshape(SEQUENCE_LENGTH, KEY_VALUE_HEADS, group_width, HEAD_SIZE)
    key_head_rows = key_token_rows.astype(jnp.float32).reshape(SEQUENCE_LENGTH, KEY_VALUE_HEADS, HEAD_SIZE)
    value_head_rows = value_token_rows.astype(jnp.float32).reshape(SEQUENCE_LENGTH, KEY_VALUE_HEADS, HEAD_SIZE)
    scores = jnp.einsum("qagd,kad->agqk", query_head_rows, key_head_rows) * score_scale
    positions = jnp.arange(SEQUENCE_LENGTH, dtype=jnp.int32)
    allowed = positions[None, :] <= positions[:, None]
    scores = jnp.where(allowed, scores, -jnp.inf)
    top_score = jnp.max(scores, axis=-1, keepdims=True)
    raised = jnp.exp(scores - top_score)
    softmax = raised / jnp.sum(raised, axis=-1, keepdims=True)
    soft_bf = lax.optimization_barrier(softmax.astype(jnp.bfloat16))
    soft_back = soft_bf.astype(jnp.float32)
    attended = jnp.einsum("agqk,kad->qagd", soft_back, value_head_rows).astype(jnp.bfloat16)
    soft_grad = jnp.einsum("qagd,kad->agqk", gradient_heads, value_head_rows)
    row_dots = jnp.sum(softmax * soft_grad, axis=-1, keepdims=True)
    score_grad = lax.optimization_barrier((softmax * (soft_grad - row_dots)).astype(jnp.bfloat16))
    score_back = score_grad.astype(jnp.float32)
    query_grad = (jnp.einsum("agqk,kad->qagd", score_back, key_head_rows) * score_scale).astype(jnp.bfloat16)
    key_gradient_sum = jnp.einsum("agqk,qagd->kad", score_back, query_head_rows) * score_scale
    value_gradient_sum = jnp.einsum("agqk,qagd->kad", soft_back, gradient_heads)
    return (attended.reshape(SEQUENCE_LENGTH, QUERY_HEADS * HEAD_SIZE), query_grad.reshape(SEQUENCE_LENGTH, QUERY_HEADS * HEAD_SIZE),
            key_gradient_sum.astype(jnp.bfloat16).reshape(SEQUENCE_LENGTH, KEY_VALUE_HEADS * HEAD_SIZE),
            value_gradient_sum.astype(jnp.bfloat16).reshape(SEQUENCE_LENGTH, KEY_VALUE_HEADS * HEAD_SIZE))


def reference(normed, queries, stored_keys, stored_values, upstream, query_weight, key_matrix, value_matrix, output_weight):
    block_width = MODEL_WIDTH // N_ROW
    up_blocks = upstream.reshape(TOKEN_TOTAL, N_ROW, block_width).transpose(1, 0, 2)
    out_blocks = output_weight.reshape(QUERY_HEADS * HEAD_SIZE, N_ROW, block_width).transpose(1, 0, 2)

    def add_block(running, operands):
        product = jnp.dot(operands[0], operands[1].T, preferred_element_type=jnp.float32)
        rounded = lax.optimization_barrier(product.astype(jnp.bfloat16))
        return running + rounded.astype(jnp.float32), None

    summed, _ = lax.scan(add_block, jnp.zeros((TOKEN_TOTAL, QUERY_HEADS * HEAD_SIZE), jnp.float32), (up_blocks, out_blocks))
    attended_gradient = summed.astype(jnp.bfloat16)
    sequence_list = (queries.reshape(SEQUENCE_COUNT, SEQUENCE_LENGTH, QUERY_HEADS * HEAD_SIZE), stored_keys.reshape(SEQUENCE_COUNT, SEQUENCE_LENGTH, KEY_VALUE_HEADS * HEAD_SIZE),
                 stored_values.reshape(SEQUENCE_COUNT, SEQUENCE_LENGTH, KEY_VALUE_HEADS * HEAD_SIZE), attended_gradient.reshape(SEQUENCE_COUNT, SEQUENCE_LENGTH, QUERY_HEADS * HEAD_SIZE))
    result_list = lax.map(one_sequence, sequence_list)
    attended = result_list[0].reshape(TOKEN_TOTAL, QUERY_HEADS * HEAD_SIZE)
    query_grad = result_list[1].reshape(TOKEN_TOTAL, QUERY_HEADS * HEAD_SIZE)
    key_gradient = result_list[2].reshape(TOKEN_TOTAL, KEY_VALUE_HEADS * HEAD_SIZE)
    value_gradient = result_list[3].reshape(TOKEN_TOTAL, KEY_VALUE_HEADS * HEAD_SIZE)
    grad_output = jnp.dot(attended.T, upstream, preferred_element_type=jnp.float32).astype(jnp.bfloat16)
    grad_query = jnp.dot(normed.T, query_grad, preferred_element_type=jnp.float32).astype(jnp.bfloat16)
    grad_key = jnp.dot(normed.T, key_gradient, preferred_element_type=jnp.float32).astype(jnp.bfloat16)
    grad_value = jnp.dot(normed.T, value_gradient, preferred_element_type=jnp.float32).astype(jnp.bfloat16)
    grad_normed = (jnp.dot(query_grad, query_weight.T, preferred_element_type=jnp.float32)
                   + jnp.dot(key_gradient, key_matrix.T, preferred_element_type=jnp.float32)
                   + jnp.dot(value_gradient, value_matrix.T, preferred_element_type=jnp.float32)).astype(jnp.bfloat16)
    return (grad_normed, grad_query, grad_key, grad_value, grad_output)
```

```python
import functools

import jax
import jax.numpy as jnp
from jax import lax
from jax.experimental import pallas as pl
from jax.experimental.pallas import tpu as pltpu
from jax.sharding import PartitionSpec as P

QUERY_HEADS = 64
KEY_VALUE_HEADS = 8
HEAD_SIZE = 128
SEQUENCE_LENGTH = 256
SCALE = HEAD_SIZE ** (-0.5)
LOG2E = 1.4426950408889634
F32 = jnp.float32
BF = jnp.bfloat16
PARAMS = pltpu.CompilerParams(vmem_limit_bytes=24 * 1024 * 1024)
CONTRACT_LAST = (((1,), (1,)), ((), ()))

def probabilities(keys, head_queries, allowed):
    scores = lax.dot_general(keys, head_queries, CONTRACT_LAST, preferred_element_type=F32)
    scores = jnp.where(allowed, scores, -jnp.inf)
    top = jnp.max(scores, axis=0, keepdims=True)
    raised = jnp.exp2((scores - top) * (SCALE * LOG2E))
    total = jnp.sum(raised, axis=0, keepdims=True)
    return raised * (1.0 / total)

def causal():
    shape=(SEQUENCE_LENGTH, SEQUENCE_LENGTH)
    return lax.broadcasted_iota(jnp.int32, shape, 0) <= lax.broadcasted_iota(jnp.int32, shape, 1)

def forward_kernel(heads, q_ref, k_ref, v_ref, o_ref):
    allowed = causal()
    keys = k_ref[...]
    values_t = v_ref[...].T
    for h in range(heads):
        cols = slice(h*HEAD_SIZE,(h+1)*HEAD_SIZE)
        soft = probabilities(keys, q_ref[:, cols], allowed).astype(BF)
        o_ref[cols, :] = jnp.dot(values_t, soft, preferred_element_type=F32).astype(BF)

def attended_transposed(queries, keys, values):
    tokens, width = queries.shape
    kv = keys.shape[1]//HEAD_SIZE
    gw = width//kv
    L = SEQUENCE_LENGTH
    return pl.pallas_call(
        functools.partial(forward_kernel, gw//HEAD_SIZE),
        grid=(tokens//L, kv),
        in_specs=[pl.BlockSpec((L,gw),lambda s,g:(s,g)),
                  pl.BlockSpec((L,HEAD_SIZE),lambda s,g:(s,g)),
                  pl.BlockSpec((L,HEAD_SIZE),lambda s,g:(s,g))],
        out_specs=pl.BlockSpec((gw,L),lambda s,g:(g,s)),
        out_shape=jax.ShapeDtypeStruct((width,tokens),BF),
        compiler_params=PARAMS,
        name="attention_forward",
        cost_estimate=pl.CostEstimate(flops=4*tokens*L*width, bytes_accessed=4*tokens*width, transcendentals=0),
    )(queries,keys,values)

def backward_kernel(k, heads, pieces, fresh, place_ref, q_ref, k_ref, v_ref, *rest):
    piece_refs = rest[:pieces]
    if fresh:
        dq_ref, dk_ref, dv_ref, grad_ref = rest[pieces:]
    else:
        _, dk_in, dv_in, dq_ref, dk_ref, dv_ref, grad_ref = rest[pieces:]
    s = pl.program_id(0)
    L = SEQUENCE_LENGTH

    @pl.when(s == 0)
    def _():
        j = 0
        for ref in piece_refs:
            rows = ref.shape[0] if ref.shape[0] * 4 == grad_ref.shape[0] else ref.shape[0] // 2
            for start in range(0, ref.shape[0], rows):
                offset = pl.multiple_of(place_ref[12 + j], 64)
                grad_ref[pl.ds(offset, rows), :] = ref[start : start + rows, :]
                j += 1

    allowed = causal()
    keys = k_ref[...]
    values = v_ref[...]
    keys_t = keys.T
    row = pl.multiple_of(s * L, L)
    dk = jnp.zeros((L, HEAD_SIZE), F32)
    dv = jnp.zeros((L, HEAD_SIZE), F32)
    for h in range(heads):
        cols = slice(h * HEAD_SIZE, (h + 1) * HEAD_SIZE)
        hq = q_ref[:, cols]
        hg = grad_ref[pl.ds(row, L), cols]
        soft = probabilities(keys, hq, allowed)
        soft_grad = lax.dot_general(values, hg, CONTRACT_LAST, preferred_element_type=F32)
        dots = jnp.sum(soft * soft_grad, axis=0, keepdims=True)
        score_grad = (soft * (soft_grad - dots)).astype(BF)
        dv += jnp.dot(soft.astype(BF), hg, preferred_element_type=F32)
        dk += jnp.dot(score_grad, hq, preferred_element_type=F32) * SCALE
        dq_t = jnp.dot(keys_t, score_grad, preferred_element_type=F32) * SCALE
        dq_ref[:, cols] = dq_t.T.astype(BF)
    if fresh:
        dk_ref[...] = dk
        dv_ref[...] = dv
    else:
        again = place_ref[8 + k] != 0
        dk_ref[...] = jnp.where(again, dk_in[...] + dk, dk)
        dv_ref[...] = jnp.where(again, dv_in[...] + dv, dv)


def attention_backward(k, place, queries, keys, values, pieces, earlier):
    tokens, width = queries.shape
    quarter = pieces[0].shape[1]
    L = SEQUENCE_LENGTH
    small = pl.BlockSpec((L, HEAD_SIZE), lambda s, place: (s, place[4 + k]))
    wide = pl.BlockSpec((L, quarter), lambda s, place: (s, place[k]))
    n = len(pieces)
    fresh = earlier is None
    spec = pltpu.PrefetchScalarGridSpec(
        num_scalar_prefetch=1,
        grid=(tokens // L,),
        in_specs=[wide, small, small]
        + [pl.BlockSpec(x.shape, lambda s, place: (0, 0)) for x in pieces]
        + ([] if fresh else [pl.BlockSpec(memory_space=pl.ANY), small, small]),
        out_specs=[wide, small, small],
        scratch_shapes=[pltpu.VMEM((tokens, quarter), BF)],
    )
    sums = jax.ShapeDtypeStruct(keys.shape, F32)
    return pl.pallas_call(
        functools.partial(backward_kernel, k, quarter // HEAD_SIZE, n, fresh),
        grid_spec=spec,
        out_shape=[jax.ShapeDtypeStruct(queries.shape, BF), sums, sums],
        input_output_aliases={} if fresh else {4 + n: 0, 5 + n: 1, 6 + n: 2},
        compiler_params=PARAMS,
        name="attention_backward",
        cost_estimate=pl.CostEstimate(flops=60 * tokens * L * quarter, bytes_accessed=8 * tokens * quarter, transcendentals=0),
    )(place, queries, keys, values, *pieces, *([] if fresh else earlier))


def partial_kernel(order_ref, first_ref, second_ref, weight_ref, low_ref, high_ref, near_ref, far_ref, own_ref, both_ref):
    step = pl.program_id(0)
    rows = first_ref.shape[0]

    @pl.when(step == 0)
    def _():
        both_ref[:rows, :] = first_ref[...]
        both_ref[rows:, :] = second_ref[...]

    product = lax.dot_general(both_ref[...], weight_ref[...], CONTRACT_LAST, preferred_element_type=F32).astype(BF)

    @pl.when(step == 0)
    def _():
        low_ref[...] = product[:rows, :]
        high_ref[...] = product[rows:, :]

    for place, out_ref in ((1, near_ref), (2, far_ref), (3, own_ref)):
        @pl.when(step == place)
        def _(out_ref=out_ref):
            out_ref[...] = product


def partial_products(order, first, second, weight):
    rows, features = first.shape
    quarter = weight.shape[0] // 4
    half = jax.ShapeDtypeStruct((rows, quarter), BF)
    full = jax.ShapeDtypeStruct((2 * rows, quarter), BF)
    same = lambda shape: pl.BlockSpec(shape, lambda k, order: (0, 0))
    spec = pltpu.PrefetchScalarGridSpec(
        num_scalar_prefetch=1,
        grid=(4,),
        in_specs=[same(first.shape), same(second.shape), pl.BlockSpec((quarter, features), lambda k, order: (order[k], 0))],
        out_specs=[same(half.shape)] * 2 + [same(full.shape)] * 3,
        scratch_shapes=[pltpu.VMEM((2 * rows, features), BF)],
    )
    return pl.pallas_call(
        partial_kernel,
        grid_spec=spec,
        out_shape=[half] * 2 + [full] * 3,
        compiler_params=PARAMS,
        name="gradient_partial",
        cost_estimate=pl.CostEstimate(
            flops=16 * rows * features * quarter,
            bytes_accessed=2 * (2 * rows * features + 4 * quarter * features + 8 * rows * quarter),
            transcendentals=0,
        ),
    )(order, first, second, weight)


def weights_kernel(n_ref, dq_ref, dk_ref, dv_ref, gq_ref, gk_ref, gv_ref):
    nt = n_ref[...].T
    gq_ref[...] = jnp.dot(nt, dq_ref[...], preferred_element_type=F32).astype(BF)
    gk_ref[...] = jnp.dot(nt, dk_ref[...].astype(BF), preferred_element_type=F32).astype(BF)
    gv_ref[...] = jnp.dot(nt, dv_ref[...].astype(BF), preferred_element_type=F32).astype(BF)

def weight_gradients(normed, dq, dk, dv, block=256):
    tokens, feats = normed.shape
    whole = lambda x: pl.BlockSpec(x.shape, lambda i:(0,0))
    out = lambda x: pl.BlockSpec((block,x.shape[1]), lambda i:(i,0))
    return pl.pallas_call(
        weights_kernel, grid=(feats//block,),
        in_specs=[pl.BlockSpec((tokens,block),lambda i:(0,i)),whole(dq),whole(dk),whole(dv)],
        out_specs=[out(dq),out(dk),out(dv)],
        out_shape=[jax.ShapeDtypeStruct((feats,x.shape[1]),BF) for x in (dq,dk,dv)],
        compiler_params=PARAMS, name="weight_gradients",
        cost_estimate=pl.CostEstimate(flops=2*tokens*feats*(dq.shape[1]+2*dk.shape[1]), bytes_accessed=2*(tokens*feats*2+feats*(dq.shape[1]+512)), transcendentals=0),
    )(normed,dq,dk,dv)

def input_kernel(half, place_ref, dq_ref, dk_ref, dv_ref, wq_ref, wk_ref, wv_ref, first_ref, second_ref, total_ref):
    rows = first_ref.shape[0]
    here = pl.ds(pl.multiple_of(place_ref[16 + half], 2 * rows), 2 * rows)
    total = lax.dot_general(dq_ref[here, :], wq_ref[...], CONTRACT_LAST, preferred_element_type=F32)
    total += lax.dot_general(dk_ref[here, :].astype(BF), wk_ref[...], CONTRACT_LAST, preferred_element_type=F32)
    total += lax.dot_general(dv_ref[here, :].astype(BF), wv_ref[...], CONTRACT_LAST, preferred_element_type=F32)
    total_ref[...] = total.astype(BF)
    first_ref[...] = total_ref[pl.ds(pl.multiple_of(place_ref[18], rows), rows), :]
    second_ref[...] = total_ref[pl.ds(pl.multiple_of(place_ref[19], rows), rows), :]


def input_gradients(half, place, rows, dq, dk, dv, query_weight, key_matrix, value_matrix, block=512):
    features, width = query_weight.shape
    small = key_matrix.shape[1]
    whole = lambda x: pl.BlockSpec(x.shape, lambda i, place: (0, 0))
    strip = lambda x: pl.BlockSpec((block, x.shape[1]), lambda i, place: (i, 0))
    spec = pltpu.PrefetchScalarGridSpec(
        num_scalar_prefetch=1,
        grid=(features // block,),
        in_specs=[whole(dq), whole(dk), whole(dv), strip(query_weight), strip(key_matrix), strip(value_matrix)],
        out_specs=[pl.BlockSpec((rows, block), lambda i, place: (0, i))] * 2,
        scratch_shapes=[pltpu.VMEM((2 * rows, block), BF)],
    )
    return pl.pallas_call(
        functools.partial(input_kernel, half),
        grid_spec=spec,
        out_shape=[jax.ShapeDtypeStruct((rows, features), BF)] * 2,
        compiler_params=PARAMS,
        name="input_gradients",
        cost_estimate=pl.CostEstimate(
            flops=4 * rows * features * (width + 2 * small),
            bytes_accessed=2 * ((features + dq.shape[0]) * (width + 2 * small) + 2 * rows * features),
            transcendentals=0,
        ),
    )(place, dq, dk, dv, query_weight, key_matrix, value_matrix)

def attend(query_token_rows, key_token_rows, value_token_rows, gradient_rows):
    token_count = query_token_rows.shape[0]
    kv_groups = key_token_rows.shape[1] // HEAD_SIZE
    group_width = QUERY_HEADS // KEY_VALUE_HEADS
    score_scale = HEAD_SIZE ** (-0.5)
    query_head_rows = query_token_rows.reshape(token_count, kv_groups, group_width, HEAD_SIZE)
    gradient_heads = gradient_rows.reshape(token_count, kv_groups, group_width, HEAD_SIZE)
    key_head_rows = key_token_rows.reshape(token_count, kv_groups, HEAD_SIZE)
    value_head_rows = value_token_rows.reshape(token_count, kv_groups, HEAD_SIZE)
    scores = (
        jnp.einsum(
            "qagd,kad->agqk", query_head_rows, key_head_rows, preferred_element_type=jnp.float32
        )
        * score_scale
    )
    positions = jnp.arange(token_count, dtype=jnp.int32)
    allowed = positions[None, :] <= positions[:, None]
    scores = jnp.where(allowed, scores, -jnp.inf)
    top_score = jnp.max(scores, axis=-1, keepdims=True)
    raised = jnp.exp(scores - top_score)
    softmax = raised / jnp.sum(raised, axis=-1, keepdims=True)
    soft_bf = softmax.astype(jnp.bfloat16)
    attended = jnp.einsum(
        "agqk,kad->qagd", soft_bf, value_head_rows, preferred_element_type=jnp.float32
    )
    attended = attended.astype(jnp.bfloat16).reshape(token_count, -1)
    soft_grad = jnp.einsum(
        "qagd,kad->agqk", gradient_heads, value_head_rows, preferred_element_type=jnp.float32
    )
    row_dots = jnp.sum(softmax * soft_grad, axis=-1, keepdims=True)
    score_grad = (softmax * (soft_grad - row_dots)).astype(jnp.bfloat16)
    query_grad = (
        jnp.einsum("agqk,kad->qagd", score_grad, key_head_rows, preferred_element_type=jnp.float32)
        * score_scale
    )
    query_grad = query_grad.astype(jnp.bfloat16).reshape(token_count, -1)
    key_gradient = (
        jnp.einsum(
            "agqk,qagd->kad", score_grad, query_head_rows, preferred_element_type=jnp.float32
        )
        * score_scale
    )
    value_gradient = jnp.einsum(
        "agqk,qagd->kad", soft_bf, gradient_heads, preferred_element_type=jnp.float32
    )
    return (
        attended,
        query_grad,
        key_gradient.reshape(token_count, -1),
        value_gradient.reshape(token_count, -1),
    )


def general_shards(
    normed,
    queries,
    stored_keys,
    stored_values,
    upstream,
    query_weight,
    key_matrix,
    value_matrix,
    output_weight,
):
    tokens = stored_keys.shape[0]
    normed_all, upstream_all = (
        lax.all_gather(normed, ("col", "sub"), axis=0, tiled=True),
        lax.all_gather(upstream, ("col", "sub"), axis=0, tiled=True),
    )
    contract_last = (((1,), (1,)), ((), ()))
    contract_first = (((0,), (0,)), ((), ()))
    partial_sum = lax.dot_general(
        upstream_all, output_weight, contract_last, preferred_element_type=jnp.float32
    )
    attended_gradient = lax.psum(partial_sum.astype(jnp.bfloat16), "row")
    query_token_rows = lax.all_gather(queries, "row", axis=0, tiled=True)
    sequence_list = tokens // SEQUENCE_LENGTH

    def per_sequence(blocks):
        return attend(blocks[0], blocks[1], blocks[2], blocks[3])

    result_list = lax.map(
        per_sequence,
        (
            query_token_rows.reshape(sequence_list, SEQUENCE_LENGTH, -1),
            stored_keys.reshape(sequence_list, SEQUENCE_LENGTH, -1),
            stored_values.reshape(sequence_list, SEQUENCE_LENGTH, -1),
            attended_gradient.reshape(sequence_list, SEQUENCE_LENGTH, -1),
        ),
    )
    attended_all = result_list[0].reshape(tokens, -1)
    query_all = result_list[1].reshape(tokens, -1)
    key_all = result_list[2].reshape(tokens, -1).astype(jnp.bfloat16)
    value_all = result_list[3].reshape(tokens, -1).astype(jnp.bfloat16)
    grad_output = lax.dot_general(
        attended_all, upstream_all, contract_first, preferred_element_type=jnp.float32
    ).astype(jnp.bfloat16)
    grad_query = lax.dot_general(
        normed_all, query_all, contract_first, preferred_element_type=jnp.float32
    ).astype(jnp.bfloat16)
    grad_key = lax.dot_general(
        normed_all, key_all, contract_first, preferred_element_type=jnp.float32
    ).astype(jnp.bfloat16)
    grad_value = lax.dot_general(
        normed_all, value_all, contract_first, preferred_element_type=jnp.float32
    ).astype(jnp.bfloat16)
    summed = lax.dot_general(
        query_all, query_weight, contract_last, preferred_element_type=jnp.float32
    )
    summed = summed + lax.dot_general(
        key_all, key_matrix, contract_last, preferred_element_type=jnp.float32
    )
    grad_normed = lax.psum_scatter(
        (
            summed
            + lax.dot_general(
                value_all, value_matrix, contract_last, preferred_element_type=jnp.float32
            )
        ).astype(jnp.bfloat16),
        ("col", "sub"),
        scatter_dimension=0,
        tiled=True,
    )
    return (grad_normed, grad_query, grad_key, grad_value, grad_output)


def swap(x, axis):
    return lax.ppermute(x, axis, [(0, 1), (1, 0)])


def turn(x, step, n):
    return lax.ppermute(x, "row", [(i, (i + step) % n) for i in range(n)])


def shift(x, step, done, n):
    pairs = [(i, i + step) for i in range(n) if 0 <= i + step < n and 0 <= i - done * step < n]
    return lax.ppermute(x, "row", pairs)


def after(value, others):
    return lax.optimization_barrier((value, others))


def total(mine, from_left, from_right):
    return (mine.astype(F32) + from_left.astype(F32) + from_right.astype(F32)).astype(BF)


def with_arrived(products, hops):
    rows = products[0].shape[0]
    near = jnp.concatenate([products[2][:rows], products[2][rows:] + hops[0]])
    far = jnp.concatenate([products[3][:rows] + hops[1], products[3][rows:]])
    return near, far


def in_place(parts, here, rows):
    whole = jnp.zeros((len(parts) * rows, parts[0].shape[1]), parts[0].dtype)
    for j, part in enumerate(parts):
        whole = lax.dynamic_update_slice(whole, part, (rows * (here ^ j), 0))
    return whole


def shards(
    normed,
    queries,
    stored_keys,
    stored_values,
    upstream,
    query_weight,
    key_matrix,
    value_matrix,
    output_weight,
):
    row = lax.axis_index("row")
    col = lax.axis_index("col")
    sub = lax.axis_index("sub")
    here = 2 * col + sub
    rows = upstream.shape[0]
    quarters = [(row + k) % 4 for k in range(4)]
    order = jnp.stack([quarters[2], quarters[1], quarters[3], quarters[0]]).astype(jnp.int32)
    visited = [0 * row, 1 - row % 2, 0 * row + 1, row % 2]
    places = jnp.stack(
        quarters
        + [quarter // 2 for quarter in quarters]
        + visited
        + [rows * (here ^ j) for j in range(4)]
        + [2 * rows * (1 - col), 2 * rows * col, rows * (1 - sub), rows * sub]
    ).astype(jnp.int32)

    normed_all = lax.all_gather(normed, ("col", "sub"), axis=0, tiled=True)
    ups = [upstream, swap(upstream, "sub"), swap(upstream, "col")]
    onward_right, onward_left = queries, queries
    from_lefts, from_rights = [], []
    for hop in range(3):
        onward_right = shift(onward_right, 1, hop, 4)
        onward_left = shift(onward_left, -1, hop, 4)
        from_lefts.append(onward_right)
        from_rights.append(onward_left)

    first = partial_products(order, ups[0], ups[1], output_weight)
    first_hops = turn(first[1], 1, 4), turn(first[0], -1, 4)
    ups[2], first = after(ups[2], first)
    ups.append(swap(ups[2], "sub"))
    second = partial_products(order, ups[2], ups[3], output_weight)
    second_hops = turn(second[1], 1, 4), turn(second[0], -1, 4)
    first_hops, second = after(first_hops, second)
    first_sums = with_arrived(first, first_hops)
    first_hops = turn(first_sums[0], 1, 4), turn(first_sums[1], -1, 4)
    second_hops, first_sums = after(second_hops, first_sums)
    second_sums = with_arrived(second, second_hops)
    second_hops = turn(second_sums[0], 1, 4), turn(second_sums[1], -1, 4)
    (from_lefts, from_rights, ups), second_sums = after((from_lefts, from_rights, ups), second_sums)
    query_all = jnp.zeros((4 * rows, queries.shape[1]), BF)
    query_all = lax.dynamic_update_slice(query_all, queries, (rows * row, 0))
    for k in range(1, 4):
        part = jnp.where(row >= k, from_lefts[k - 1], from_rights[3 - k])
        query_all = lax.dynamic_update_slice(query_all, part, (rows * quarters[-k], 0))
    attended = attended_transposed(query_all, stored_keys, stored_values)
    upstream_all = in_place(ups, here, rows)
    first_hops, (attended, upstream_all) = after(first_hops, (attended, upstream_all))
    own = [total(first[4], *first_hops)]
    left = [turn(own[0], 1, 4)]
    right = [turn(own[0], -1, 4)]
    second_hops, own = after(second_hops, own)
    own.append(total(second[4], *second_hops))
    left.append(turn(own[1], 1, 4))
    right.append(turn(own[1], -1, 4))

    def backward(k, pieces, results):
        return attention_backward(k, places, query_all, stored_keys, stored_values, pieces, results)

    results = backward(0, own, None)
    (attended, upstream_all), results = after((attended, upstream_all), results)
    grad_output = jnp.dot(attended, upstream_all, preferred_element_type=F32).astype(BF)
    (left, right), (results, grad_output) = after((left, right), (results, grad_output))
    onward = []
    for a, b in zip(left, right):
        onward += [a[:rows], b[rows:]]
    (left, right), onward = after((left, right), onward)
    opposite = [turn(x, 1 if i % 2 == 0 else -1, 4) for i, x in enumerate(onward)]
    results = backward(1, right, results)
    results = backward(3, left, results)
    opposite, results = after(opposite, results)
    query_grad, key_grad, value_grad = backward(2, opposite, results)

    weights = (query_grad, key_grad, value_grad, query_weight, key_matrix, value_matrix)
    to_sub, to_col = input_gradients(0, places, rows, *weights)
    to_col = to_col + swap(to_sub, "sub")
    from_col = swap(to_col, "col")
    weights, to_col = after(weights, to_col)
    to_sub, kept = input_gradients(1, places, rows, *weights)
    from_sub = swap(to_sub, "sub")
    grad_query, grad_key, grad_value = weight_gradients(normed_all, *weights[:3], block=512)
    (from_col, from_sub), grad_query = after((from_col, from_sub), grad_query)
    grad_normed = (kept.astype(F32) + from_sub.astype(F32) + from_col.astype(F32)).astype(BF)
    return (grad_normed, grad_query, grad_key, grad_value, grad_output)


def solution(mesh):
    in_specs = (
        P(("groups", "col", "sub"), "row"),
        P(("groups", "row"), ("col", "sub")),
        P("groups", ("col", "sub")),
        P("groups", ("col", "sub")),
        P(("groups", "col", "sub"), "row"),
        P(("groups", "row"), ("col", "sub")),
        P(("groups", "row"), ("col", "sub")),
        P(("groups", "row"), ("col", "sub")),
        P(("groups", "col", "sub"), "row"),
    )
    out_specs = (
        P(("groups", "col", "sub"), "row"),
        P(("groups", "row"), ("col", "sub")),
        P(("groups", "row"), ("col", "sub")),
        P(("groups", "row"), ("col", "sub")),
        P(("groups", "col", "sub"), "row"),
    )
    small = tuple(mesh.shape[axis] for axis in ("row", "col", "sub")) == (4, 2, 2)
    return jax.shard_map(shards if small else general_shards, mesh=mesh, in_specs=in_specs, out_specs=out_specs, check_vma=False)
```

```python
import functools

import jax
import jax.numpy as jnp
from jax import lax
from jax.experimental import pallas as pl
from jax.experimental.pallas import tpu as pltpu
from jax.sharding import PartitionSpec as P

QUERY_HEADS = 64
KEY_VALUE_HEADS = 8
HEAD_SIZE = 128
SEQUENCE_LENGTH = 256
SCALE = HEAD_SIZE ** (-0.5)
LOG2E = 1.4426950408889634
F32 = jnp.float32
BF = jnp.bfloat16
PLACE_SEND, PLACE_HEAD, PLACE_KEY, PLACE_BLOCK, PLACE_HALF, PLACE_SUB, PLACE_END, PLACE_PART, PLACE_TURN = 0, 4, 8, 12, 16, 18, 20, 21, 25
SEND_ORDER = ((3, 2, 1, 0), (3, 2, 0, 1), (0, 1, 3, 2), (0, 1, 2, 3))
TURN_ORDER = ((0, 1, 2), (0, 1, 2), (2, 1, 0), (2, 1, 0))
HEAD_ORDER = ((0, 1, 2, 3), (1, 0, 2, 3), (2, 3, 1, 0), (3, 2, 1, 0))
BLOCK = 128
GROUP = 4
COST = pl.CostEstimate(flops=1 << 20, bytes_accessed=1 << 16, transcendentals=0)
STREAMED = pltpu.CompilerParams(vmem_limit_bytes=60 * 1024 * 1024)
PARAMS = pltpu.CompilerParams(vmem_limit_bytes=24 * 1024 * 1024)
SMALL = pltpu.CompilerParams(vmem_limit_bytes=12 * 1024 * 1024)
CONTRACT_LAST = (((1,), (1,)), ((), ()))

def probabilities(keys, stacked, start):
    scores = lax.dot_general(keys, stacked, CONTRACT_LAST, preferred_element_type=F32)
    shape = (BLOCK, stacked.shape[0])
    allowed = lax.broadcasted_iota(jnp.int32, shape, 0) <= lax.broadcasted_iota(jnp.int32, shape, 1) % BLOCK
    diagonal = jnp.where(allowed, scores[start:], -jnp.inf)
    scores = jnp.concatenate([scores[:start], diagonal]) if start else diagonal
    top = jnp.max(scores, axis=0, keepdims=True)
    raised = jnp.exp2((scores - top) * (SCALE * LOG2E))
    total = jnp.sum(raised, axis=0, keepdims=True)
    return raised * (1.0 / total)


def stack(ref, rows, heads):
    return jnp.concatenate([ref[rows, h * HEAD_SIZE : (h + 1) * HEAD_SIZE] for h in range(heads)])


def assemble(place_ref, refs, groups, whole_ref):
    rows = whole_ref.shape[0] // 4

    def put(ref, at):
        whole_ref[pl.ds(pl.multiple_of(place_ref[PLACE_PART + at], 64), rows), :] = ref[...]

    first = 0
    for at, count in enumerate(groups):
        if count == 1:
            put(refs[first], at)
        else:
            for choice in range(2):
                pl.when(place_ref[PLACE_END] == 1 - choice)(functools.partial(put, refs[first + choice], at))
        first += count


def forward_kernel(groups, turn, earlier, place_ref, *refs):
    parts, refs = refs[: sum(groups)], refs[sum(groups) :]
    k_ref, v_ref = refs[:2]
    o_ref, whole_ref = refs[2 + earlier :]
    step = pl.program_id(1)
    heads = whole_ref.shape[1] // HEAD_SIZE

    @pl.when(step == 0)
    def _():
        assemble(place_ref, parts, groups, whole_ref)

    keys = k_ref[...]
    values_t = v_ref[...].T
    base = place_ref[PLACE_TURN + turn + step] * SEQUENCE_LENGTH
    for start in range(0, SEQUENCE_LENGTH, BLOCK):
        stop = start + BLOCK
        here = pl.ds(pl.multiple_of(base + start, BLOCK), BLOCK)
        for first in range(0, heads, GROUP):
            stacked = jnp.concatenate(
                [whole_ref[here, h * HEAD_SIZE : (h + 1) * HEAD_SIZE] for h in range(first, first + GROUP)]
            )
            soft = probabilities(keys[:stop], stacked, start).astype(BF)
            attended = jnp.dot(values_t[:, :stop], soft, preferred_element_type=F32).astype(BF)
            for n in range(GROUP):
                h = first + n
                o_ref[h * HEAD_SIZE : (h + 1) * HEAD_SIZE, start:stop] = attended[:, n * BLOCK : (n + 1) * BLOCK]


def attended_transposed(place, parts, keys, values, turn, count, earlier=()):
    flat = [x for part in parts for x in part]
    rows, width = flat[0].shape
    tokens = keys.shape[0]
    kv = keys.shape[1] // HEAD_SIZE
    each = width // kv
    L = SEQUENCE_LENGTH
    small = pl.BlockSpec((L, HEAD_SIZE), lambda g, s, place: (place[PLACE_TURN + turn + s], g))
    spec = pltpu.PrefetchScalarGridSpec(
        num_scalar_prefetch=1,
        grid=(kv, count),
        in_specs=[pl.BlockSpec((rows, each), lambda g, s, place: (0, g))] * len(flat)
        + [small, small]
        + [pl.BlockSpec(memory_space=pl.ANY)] * len(earlier),
        out_specs=pl.BlockSpec((each, L), lambda g, s, place: (g, place[PLACE_TURN + turn + s])),
        scratch_shapes=[pltpu.VMEM((4 * rows, each), BF)],
    )
    return pl.pallas_call(
        functools.partial(forward_kernel, [len(part) for part in parts], turn, len(earlier)),
        grid_spec=spec,
        out_shape=jax.ShapeDtypeStruct((width, tokens), BF),
        input_output_aliases={3 + len(flat): 0} if earlier else {},
        compiler_params=SMALL,
        name="attention_forward",
        cost_estimate=COST,
    )(place, *flat, keys, values, *earlier)


def backward_kernel(slot, heads, groups, counts, place_ref, k_ref, v_ref, *rest):
    parts, rest = rest[: sum(counts)], rest[sum(counts) :]
    pieces, rest = rest[: sum(groups)], rest[sum(groups) :]
    if slot == 0:
        dq_ref, dk_ref, dv_ref, grad_ref, q_ref = rest
    else:
        _, dk_in, dv_in, dq_ref, dk_ref, dv_ref, grad_ref, q_ref = rest
    s = pl.program_id(0)
    L = SEQUENCE_LENGTH
    rows = grad_ref.shape[0] // 4

    def put(ref, chunk):
        for j in range(2):
            offset = pl.multiple_of(place_ref[PLACE_BLOCK + 2 * chunk + j], 64)
            grad_ref[pl.ds(offset, rows), :] = ref[j * rows : (j + 1) * rows, :]

    @pl.when(s == 0)
    def _():
        assemble(place_ref, parts, counts, q_ref)
        at = 0
        for chunk, count in enumerate(groups):
            if count == 1:
                put(pieces[at], chunk)
            else:
                for choice in range(2):
                    pl.when(place_ref[PLACE_END] == 1 - choice)(functools.partial(put, pieces[at + choice], chunk))
            at += count

    keys = k_ref[...]
    values = v_ref[...]
    keys_t = keys.T
    dk_ref[...] = dk_in[...] if slot % 2 else jnp.zeros((L, HEAD_SIZE), F32)
    dv_ref[...] = dv_in[...] if slot % 2 else jnp.zeros((L, HEAD_SIZE), F32)
    for start in range(0, L, BLOCK):
        stop = start + BLOCK
        here = pl.ds(pl.multiple_of(s * L + start, BLOCK), BLOCK)
        stacked = stack(q_ref, here, heads)
        grads = stack(grad_ref, here, heads)
        soft = probabilities(keys[:stop], stacked, start)
        soft_grad = lax.dot_general(values[:stop], grads, CONTRACT_LAST, preferred_element_type=F32)
        dots = jnp.sum(soft * soft_grad, axis=0, keepdims=True)
        score_grad = (soft * (soft_grad - dots)).astype(BF)
        dv_ref[:stop, :] += jnp.dot(soft.astype(BF), grads, preferred_element_type=F32)
        dk_ref[:stop, :] += jnp.dot(score_grad, stacked, preferred_element_type=F32) * SCALE
        dq_t = (jnp.dot(keys_t[:, :stop], score_grad, preferred_element_type=F32) * SCALE).astype(BF)
        for h in range(heads):
            dq_ref[start:stop, h * HEAD_SIZE : (h + 1) * HEAD_SIZE] = dq_t[:, h * BLOCK : (h + 1) * BLOCK].T


def attention_backward(slot, place, parts, keys, values, chunks, earlier):
    flat = [x for part in parts for x in part]
    pieces = [piece for chunk in chunks for piece in chunk]
    rows, width = flat[0].shape
    tokens = keys.shape[0]
    quarter = pieces[0].shape[1]
    L = SEQUENCE_LENGTH
    small = pl.BlockSpec((L, HEAD_SIZE), lambda s, place: (s, place[PLACE_KEY + slot]))
    wide = pl.BlockSpec((L, quarter), lambda s, place: (s, place[PLACE_HEAD + slot]))
    n = len(pieces) + len(flat)
    spec = pltpu.PrefetchScalarGridSpec(
        num_scalar_prefetch=1,
        grid=(tokens // L,),
        in_specs=[small, small]
        + [pl.BlockSpec((rows, quarter), lambda s, place: (0, place[PLACE_HEAD + slot]))] * len(flat)
        + [pl.BlockSpec(x.shape, lambda s, place: (0, 0)) for x in pieces]
        + ([] if slot == 0 else [pl.BlockSpec(memory_space=pl.ANY), small, small]),
        out_specs=[wide, small, small],
        scratch_shapes=[pltpu.VMEM((tokens, quarter), BF)] * 2,
    )
    sums = jax.ShapeDtypeStruct(keys.shape, F32)
    return pl.pallas_call(
        functools.partial(
            backward_kernel,
            slot,
            quarter // HEAD_SIZE,
            [len(chunk) for chunk in chunks],
            [len(part) for part in parts],
        ),
        grid_spec=spec,
        out_shape=[jax.ShapeDtypeStruct((tokens, width), BF), sums, sums],
        input_output_aliases={} if slot == 0 else {3 + n: 0, 4 + n: 1, 5 + n: 2},
        compiler_params=SMALL,
        name="attention_backward",
        cost_estimate=COST,
    )(place, keys, values, *flat, *pieces, *([] if slot == 0 else earlier))


def partial_kernel(place_ref, first_ref, second_ref, weight_ref, far_ref, near_ref, own_ref, both_ref):
    step = pl.program_id(0)
    rows = first_ref.shape[0]

    @pl.when(step == 0)
    def _():
        both_ref[:rows, :] = first_ref[...]
        both_ref[rows:, :] = second_ref[...]

    product = lax.dot_general(both_ref[...], weight_ref[...], CONTRACT_LAST, preferred_element_type=F32).astype(BF)
    for slot, (out_ref, at) in enumerate(((far_ref, 0), (near_ref, 0), (near_ref, 2 * rows), (own_ref, 0))):
        @pl.when(step == slot)
        def _(out_ref=out_ref, at=at):
            out_ref[at : at + 2 * rows, :] = product


def partial_products(place, first, second, weight):
    rows, features = first.shape
    quarter = weight.shape[0] // 4
    shapes = [(2 * rows, quarter), (4 * rows, quarter), (2 * rows, quarter)]
    same = lambda shape: pl.BlockSpec(shape, lambda k, place: (0, 0))
    spec = pltpu.PrefetchScalarGridSpec(
        num_scalar_prefetch=1,
        grid=(4,),
        in_specs=[
            same(first.shape),
            same(second.shape),
            pl.BlockSpec((quarter, features), lambda k, place: (place[PLACE_SEND + k], 0)),
        ],
        out_specs=[same(shape) for shape in shapes],
        scratch_shapes=[pltpu.VMEM((2 * rows, features), BF)],
    )
    return pl.pallas_call(
        partial_kernel,
        grid_spec=spec,
        out_shape=[jax.ShapeDtypeStruct(shape, BF) for shape in shapes],
        compiler_params=STREAMED,
        name="gradient_partial",
        cost_estimate=COST,
    )(place, first, second, weight)


def output_kernel(attended_ref, upstream_ref, out_ref):
    out_ref[...] = jnp.dot(attended_ref[...], upstream_ref[...], preferred_element_type=F32).astype(BF)


def output_gradient(attended, upstream, block=512):
    width, tokens = attended.shape
    features = upstream.shape[1]
    return pl.pallas_call(
        output_kernel,
        grid=(width // block,),
        in_specs=[pl.BlockSpec((block, tokens), lambda i: (i, 0)), pl.BlockSpec((tokens, features), lambda i: (0, 0))],
        out_specs=pl.BlockSpec((block, features), lambda i: (i, 0)),
        out_shape=jax.ShapeDtypeStruct((width, features), BF),
        compiler_params=PARAMS,
        name="output_gradient",
        cost_estimate=COST,
    )(attended, upstream)


def weights_kernel(n_ref, dq_ref, dk_ref, dv_ref, gq_ref, gk_ref, gv_ref):
    nt = n_ref[...].T
    gq_ref[...] = jnp.dot(nt, dq_ref[...], preferred_element_type=F32).astype(BF)
    gk_ref[...] = jnp.dot(nt, dk_ref[...].astype(BF), preferred_element_type=F32).astype(BF)
    gv_ref[...] = jnp.dot(nt, dv_ref[...].astype(BF), preferred_element_type=F32).astype(BF)

def weight_gradients(normed, dq, dk, dv, block=256):
    tokens, feats = normed.shape
    whole = lambda x: pl.BlockSpec(x.shape, lambda i:(0,0))
    out = lambda x: pl.BlockSpec((block,x.shape[1]), lambda i:(i,0))
    return pl.pallas_call(
        weights_kernel, grid=(feats//block,),
        in_specs=[pl.BlockSpec((tokens,block),lambda i:(0,i)),whole(dq),whole(dk),whole(dv)],
        out_specs=[out(dq),out(dk),out(dv)],
        out_shape=[jax.ShapeDtypeStruct((feats,x.shape[1]),BF) for x in (dq,dk,dv)],
        compiler_params=STREAMED, name="weight_gradients",
        cost_estimate=COST,
    )(normed,dq,dk,dv)

def input_kernel(half, place_ref, dq_ref, dk_ref, dv_ref, wq_ref, wk_ref, wv_ref, first_ref, second_ref, total_ref):
    rows = first_ref.shape[0]
    here = pl.ds(pl.multiple_of(place_ref[PLACE_HALF + half], 2 * rows), 2 * rows)
    total = lax.dot_general(dq_ref[here, :], wq_ref[...], CONTRACT_LAST, preferred_element_type=F32)
    total += lax.dot_general(dk_ref[here, :].astype(BF), wk_ref[...], CONTRACT_LAST, preferred_element_type=F32)
    total += lax.dot_general(dv_ref[here, :].astype(BF), wv_ref[...], CONTRACT_LAST, preferred_element_type=F32)
    total_ref[...] = total.astype(BF)
    first_ref[...] = total_ref[pl.ds(pl.multiple_of(place_ref[PLACE_SUB], rows), rows), :]
    second_ref[...] = total_ref[pl.ds(pl.multiple_of(place_ref[PLACE_SUB + 1], rows), rows), :]


def input_gradients(half, place, rows, dq, dk, dv, query_weight, key_matrix, value_matrix, block=512):
    features, width = query_weight.shape
    small = key_matrix.shape[1]
    whole = lambda x: pl.BlockSpec(x.shape, lambda i, place: (0, 0))
    strip = lambda x: pl.BlockSpec((block, x.shape[1]), lambda i, place: (i, 0))
    spec = pltpu.PrefetchScalarGridSpec(
        num_scalar_prefetch=1,
        grid=(features // block,),
        in_specs=[whole(dq), whole(dk), whole(dv), strip(query_weight), strip(key_matrix), strip(value_matrix)],
        out_specs=[pl.BlockSpec((rows, block), lambda i, place: (0, i))] * 2,
        scratch_shapes=[pltpu.VMEM((2 * rows, block), BF)],
    )
    return pl.pallas_call(
        functools.partial(input_kernel, half),
        grid_spec=spec,
        out_shape=[jax.ShapeDtypeStruct((rows, features), BF)] * 2,
        compiler_params=PARAMS,
        name="input_gradients",
        cost_estimate=COST,
    )(place, dq, dk, dv, query_weight, key_matrix, value_matrix)

def attend(query_token_rows, key_token_rows, value_token_rows, gradient_rows):
    token_count = query_token_rows.shape[0]
    kv_groups = key_token_rows.shape[1] // HEAD_SIZE
    group_width = QUERY_HEADS // KEY_VALUE_HEADS
    score_scale = HEAD_SIZE ** (-0.5)
    query_head_rows = query_token_rows.reshape(token_count, kv_groups, group_width, HEAD_SIZE)
    gradient_heads = gradient_rows.reshape(token_count, kv_groups, group_width, HEAD_SIZE)
    key_head_rows = key_token_rows.reshape(token_count, kv_groups, HEAD_SIZE)
    value_head_rows = value_token_rows.reshape(token_count, kv_groups, HEAD_SIZE)
    scores = (
        jnp.einsum(
            "qagd,kad->agqk", query_head_rows, key_head_rows, preferred_element_type=jnp.float32
        )
        * score_scale
    )
    positions = jnp.arange(token_count, dtype=jnp.int32)
    allowed = positions[None, :] <= positions[:, None]
    scores = jnp.where(allowed, scores, -jnp.inf)
    top_score = jnp.max(scores, axis=-1, keepdims=True)
    raised = jnp.exp(scores - top_score)
    softmax = raised / jnp.sum(raised, axis=-1, keepdims=True)
    soft_bf = softmax.astype(jnp.bfloat16)
    attended = jnp.einsum(
        "agqk,kad->qagd", soft_bf, value_head_rows, preferred_element_type=jnp.float32
    )
    attended = attended.astype(jnp.bfloat16).reshape(token_count, -1)
    soft_grad = jnp.einsum(
        "qagd,kad->agqk", gradient_heads, value_head_rows, preferred_element_type=jnp.float32
    )
    row_dots = jnp.sum(softmax * soft_grad, axis=-1, keepdims=True)
    score_grad = (softmax * (soft_grad - row_dots)).astype(jnp.bfloat16)
    query_grad = (
        jnp.einsum("agqk,kad->qagd", score_grad, key_head_rows, preferred_element_type=jnp.float32)
        * score_scale
    )
    query_grad = query_grad.astype(jnp.bfloat16).reshape(token_count, -1)
    key_gradient = (
        jnp.einsum(
            "agqk,qagd->kad", score_grad, query_head_rows, preferred_element_type=jnp.float32
        )
        * score_scale
    )
    value_gradient = jnp.einsum(
        "agqk,qagd->kad", soft_bf, gradient_heads, preferred_element_type=jnp.float32
    )
    return (
        attended,
        query_grad,
        key_gradient.reshape(token_count, -1),
        value_gradient.reshape(token_count, -1),
    )


def general_shards(
    normed,
    queries,
    stored_keys,
    stored_values,
    upstream,
    query_weight,
    key_matrix,
    value_matrix,
    output_weight,
):
    tokens = stored_keys.shape[0]
    normed_all, upstream_all = (
        lax.all_gather(normed, ("col", "sub"), axis=0, tiled=True),
        lax.all_gather(upstream, ("col", "sub"), axis=0, tiled=True),
    )
    contract_last = (((1,), (1,)), ((), ()))
    contract_first = (((0,), (0,)), ((), ()))
    partial_sum = lax.dot_general(
        upstream_all, output_weight, contract_last, preferred_element_type=jnp.float32
    )
    attended_gradient = lax.psum(partial_sum.astype(jnp.bfloat16), "row")
    query_token_rows = lax.all_gather(queries, "row", axis=0, tiled=True)
    sequence_list = tokens // SEQUENCE_LENGTH

    def per_sequence(blocks):
        return attend(blocks[0], blocks[1], blocks[2], blocks[3])

    result_list = lax.map(
        per_sequence,
        (
            query_token_rows.reshape(sequence_list, SEQUENCE_LENGTH, -1),
            stored_keys.reshape(sequence_list, SEQUENCE_LENGTH, -1),
            stored_values.reshape(sequence_list, SEQUENCE_LENGTH, -1),
            attended_gradient.reshape(sequence_list, SEQUENCE_LENGTH, -1),
        ),
    )
    attended_all = result_list[0].reshape(tokens, -1)
    query_all = result_list[1].reshape(tokens, -1)
    key_all = result_list[2].reshape(tokens, -1).astype(jnp.bfloat16)
    value_all = result_list[3].reshape(tokens, -1).astype(jnp.bfloat16)
    grad_output = lax.dot_general(
        attended_all, upstream_all, contract_first, preferred_element_type=jnp.float32
    ).astype(jnp.bfloat16)
    grad_query = lax.dot_general(
        normed_all, query_all, contract_first, preferred_element_type=jnp.float32
    ).astype(jnp.bfloat16)
    grad_key = lax.dot_general(
        normed_all, key_all, contract_first, preferred_element_type=jnp.float32
    ).astype(jnp.bfloat16)
    grad_value = lax.dot_general(
        normed_all, value_all, contract_first, preferred_element_type=jnp.float32
    ).astype(jnp.bfloat16)
    summed = lax.dot_general(
        query_all, query_weight, contract_last, preferred_element_type=jnp.float32
    )
    summed = summed + lax.dot_general(
        key_all, key_matrix, contract_last, preferred_element_type=jnp.float32
    )
    grad_normed = lax.psum_scatter(
        (
            summed
            + lax.dot_general(
                value_all, value_matrix, contract_last, preferred_element_type=jnp.float32
            )
        ).astype(jnp.bfloat16),
        ("col", "sub"),
        scatter_dimension=0,
        tiled=True,
    )
    return (grad_normed, grad_query, grad_key, grad_value, grad_output)


def swap(x, axis):
    return lax.ppermute(x, axis, [(0, 1), (1, 0)])


def inward(x):
    return lax.ppermute(x, "row", [(0, 1), (3, 2)])


def across(x):
    return lax.ppermute(x, "row", [(1, 2), (2, 1)])


def outward(x):
    return lax.ppermute(x, "row", [(1, 0), (2, 3)])


def paired(x):
    return lax.ppermute(x, "row", [(0, 1), (1, 0), (2, 3), (3, 2)])


def after(value, others):
    return lax.optimization_barrier((value, others))


def plus(*terms):
    return sum(term.astype(F32) for term in terms).astype(BF)


def shards(
    normed,
    queries,
    stored_keys,
    stored_values,
    upstream,
    query_weight,
    key_matrix,
    value_matrix,
    output_weight,
):
    row = lax.axis_index("row")
    col = lax.axis_index("col")
    sub = lax.axis_index("sub")
    here = 2 * col + sub
    rows = upstream.shape[0]
    half = 2 * rows
    is_end = (row == 0) | (row == 3)
    index = jnp.arange(PLACE_TURN + 3, dtype=jnp.int32)
    table = jnp.array(
        [
            SEND_ORDER[r]
            + HEAD_ORDER[r]
            + tuple(q // 2 for q in HEAD_ORDER[r])
            + (0,) * 9
            + tuple(rows * q for q in HEAD_ORDER[r])
            + TURN_ORDER[r]
            for r in range(4)
        ]
    )
    place = jnp.sum(jnp.where(jnp.arange(4)[:, None] == row, table, 0), axis=0).astype(jnp.int32)
    for at, value in enumerate(
        [rows * (here ^ j) for j in range(4)]
        + [half * (1 - col), half * col, rows * (1 - sub), rows * sub, is_end.astype(jnp.int32)]
    ):
        place = jnp.where(index == PLACE_BLOCK + at, value.astype(jnp.int32), place)

    def backward(slot, pieces, results):
        return attention_backward(slot, place, query_parts, stored_keys, stored_values, pieces, results)

    first_up = swap(upstream, "sub")
    query_pair = paired(queries)
    second_up = swap(upstream, "col")
    query_mid = across(queries)
    a_far, a_near, a_own = partial_products(place, upstream, first_up, output_weight)
    (query_pair, query_mid), a_far = after((query_pair, query_mid), a_far)
    query_far = across(query_pair)
    query_out = outward(query_mid)
    (second_up, normed, late_upstream, a_far, a_near), (query_pair, query_mid) = after(
        (second_up, normed, upstream, a_far, a_near), (query_pair, query_mid)
    )
    a_in0 = inward(a_far)
    a_in = inward(a_near)
    third_up = swap(second_up, "sub")
    upstream_all = lax.all_gather(late_upstream, ("col", "sub"), axis=0, tiled=True)
    normed_all = lax.all_gather(normed, ("col", "sub"), axis=0, tiled=True)
    b_far, b_near, b_own = partial_products(place, second_up, third_up, output_weight)
    b_in0 = inward(b_far)
    a_in0, b_far = after(a_in0, b_far)
    a_mid0 = across(plus(a_far, a_in0))
    query_far, a_in0 = after(query_far, a_in0)
    query_last = outward(query_far)

    (a_mid0, query_out), query_far = after((a_mid0, query_out), query_far)
    a_out = outward(plus(a_near[half:], a_mid0))
    a_in, query_far = after(a_in, query_far)
    a_mid1 = across(plus(a_near[:half], a_in[:half]))
    b_in0, a_in = after(b_in0, a_in)
    b_mid0 = across(plus(b_far, b_in0))
    b_in = inward(b_near)
    query_out, b_in0 = after(query_out, b_in0)
    some_parts = [(queries,), (query_pair,), (query_out, query_mid)]
    attended = attended_transposed(place, some_parts, stored_keys, stored_values, 0, 2)

    (a_out, a_mid1), attended = after((a_out, a_mid1), attended)
    own_a = plus(a_own, a_in[half:], a_mid1, a_out)
    pair_a = paired(own_a)
    mid_a = across(own_a)
    b_mid0, own_a = after(b_mid0, own_a)
    b_out = outward(plus(b_near[half:], b_mid0))
    b_in, b_mid0 = after(b_in, b_mid0)
    b_mid1 = across(plus(b_near[:half], b_in[:half]))

    query_parts = some_parts + [(query_last, query_far)]
    attended = attended_transposed(place, query_parts, stored_keys, stored_values, 2, 1, [attended])
    (pair_a, mid_a), attended = after((pair_a, mid_a), attended)
    far_a = across(pair_a)
    out_a = outward(mid_a)
    (attended, upstream_all), (pair_a, mid_a) = after((attended, upstream_all), (pair_a, mid_a))
    grad_output = output_gradient(attended, upstream_all)
    (b_out, b_mid1), grad_output = after((b_out, b_mid1), grad_output)
    own_b = plus(b_own, b_in[half:], b_mid1, b_out)
    pair_b = paired(own_b)
    mid_b = across(own_b)
    results = backward(0, [(own_a,), (own_b,)], None)
    (far_a, out_a), results = after((far_a, out_a), results)
    last_a = outward(far_a)

    pair_b, mid_b, results = lax.optimization_barrier((pair_b, mid_b, results))
    far_b = across(pair_b)
    out_b = outward(mid_b)
    results = backward(1, [(pair_a,), (pair_b,)], results)

    far_b, out_b, results = lax.optimization_barrier((far_b, out_b, results))
    last_b = outward(far_b)
    results = backward(2, [(out_a, mid_a), (out_b, mid_b)], results)
    (last_a, last_b), results = after((last_a, last_b), results)
    query_grad, key_grad, value_grad = backward(3, [(last_a, far_a), (last_b, far_b)], results)

    weights = (query_grad, key_grad, value_grad, query_weight, key_matrix, value_matrix)
    to_sub, to_col = input_gradients(0, place, rows, *weights)
    to_col = to_col + swap(to_sub, "sub")
    from_col = swap(to_col, "col")
    weights, to_col = after(weights, to_col)
    to_sub, kept = input_gradients(1, place, rows, *weights)
    from_sub = swap(to_sub, "sub")
    normed_all, kept = after(normed_all, kept)
    grad_query, grad_key, grad_value = weight_gradients(normed_all, query_grad, key_grad, value_grad, block=512)
    from_col, _ = after(from_col, grad_query)
    from_sub, from_col = after(from_sub, from_col)
    grad_normed = plus(kept, from_sub, from_col)
    return (grad_normed, grad_query, grad_key, grad_value, grad_output)


def solution(mesh):
    in_specs = (
        P(("groups", "col", "sub"), "row"),
        P(("groups", "row"), ("col", "sub")),
        P("groups", ("col", "sub")),
        P("groups", ("col", "sub")),
        P(("groups", "col", "sub"), "row"),
        P(("groups", "row"), ("col", "sub")),
        P(("groups", "row"), ("col", "sub")),
        P(("groups", "row"), ("col", "sub")),
        P(("groups", "col", "sub"), "row"),
    )
    out_specs = (
        P(("groups", "col", "sub"), "row"),
        P(("groups", "row"), ("col", "sub")),
        P(("groups", "row"), ("col", "sub")),
        P(("groups", "row"), ("col", "sub")),
        P(("groups", "col", "sub"), "row"),
    )
    small = tuple(mesh.shape[axis] for axis in ("row", "col", "sub")) == (4, 2, 2)
    return jax.shard_map(shards if small else general_shards, mesh=mesh, in_specs=in_specs, out_specs=out_specs, check_vma=False)
```

```python
import functools

import jax
import jax.numpy as jnp
from jax import lax
from jax.experimental import pallas as pl
from jax.experimental.pallas import tpu as pltpu
from jax.sharding import PartitionSpec as P

QUERY_HEADS = 64
KEY_VALUE_HEADS = 8
HEAD_SIZE = 128
SEQUENCE_LENGTH = 256
SCALE = HEAD_SIZE ** (-0.5)
LOG2E = 1.4426950408889634
F32 = jnp.float32
BF = jnp.bfloat16
PLACE_SEND, PLACE_HEAD, PLACE_KEY, PLACE_BLOCK, PLACE_HALF, PLACE_SUB, PLACE_END, PLACE_PART, PLACE_TURN = 0, 4, 8, 12, 16, 18, 20, 21, 25
SEND_ORDER = ((3, 2, 1, 0), (3, 2, 0, 1), (0, 1, 3, 2), (0, 1, 2, 3))
TURN_ORDER = ((0, 1, 2), (0, 1, 2), (2, 1, 0), (2, 1, 0))
HEAD_ORDER = ((0, 1, 2, 3), (1, 0, 2, 3), (2, 3, 1, 0), (3, 2, 1, 0))
BLOCK = 128
GROUP = 4
PAIR = 2
COST = pl.CostEstimate(flops=1 << 20, bytes_accessed=1 << 16, transcendentals=0)
STREAMED = pltpu.CompilerParams(vmem_limit_bytes=60 * 1024 * 1024)
PARAMS = pltpu.CompilerParams(vmem_limit_bytes=24 * 1024 * 1024)
SMALL = pltpu.CompilerParams(vmem_limit_bytes=12 * 1024 * 1024)
CONTRACT_LAST = (((1,), (1,)), ((), ()))

def probabilities(keys, stacked, start):
    scores = lax.dot_general(keys, stacked, CONTRACT_LAST, preferred_element_type=F32)
    shape = (BLOCK, stacked.shape[0])
    allowed = lax.broadcasted_iota(jnp.int32, shape, 0) <= lax.broadcasted_iota(jnp.int32, shape, 1) % BLOCK
    diagonal = jnp.where(allowed, scores[start:], -jnp.inf)
    scores = jnp.concatenate([scores[:start], diagonal]) if start else diagonal
    top = jnp.max(scores, axis=0, keepdims=True)
    raised = jnp.exp2((scores - top) * (SCALE * LOG2E))
    total = jnp.sum(raised, axis=0, keepdims=True)
    return raised * (1.0 / total)


def stack(ref, rows, first, last):
    return jnp.concatenate([ref[rows, h * HEAD_SIZE : (h + 1) * HEAD_SIZE] for h in range(first, last)])


def assemble(place_ref, refs, groups, whole_ref):
    rows = whole_ref.shape[0] // 4

    def put(ref, at):
        whole_ref[pl.ds(pl.multiple_of(place_ref[PLACE_PART + at], 64), rows), :] = ref[...]

    first = 0
    for at, count in enumerate(groups):
        if count == 1:
            put(refs[first], at)
        else:
            for choice in range(2):
                pl.when(place_ref[PLACE_END] == 1 - choice)(functools.partial(put, refs[first + choice], at))
        first += count


def forward_kernel(groups, turn, earlier, place_ref, *refs):
    parts, refs = refs[: sum(groups)], refs[sum(groups) :]
    k_ref, v_ref = refs[:2]
    o_ref, whole_ref = refs[2 + earlier :]
    step = pl.program_id(1)
    heads = whole_ref.shape[1] // HEAD_SIZE

    @pl.when(step == 0)
    def _():
        assemble(place_ref, parts, groups, whole_ref)

    keys = k_ref[...]
    values_t = v_ref[...].T
    base = place_ref[PLACE_TURN + turn + step] * SEQUENCE_LENGTH
    for start in range(0, SEQUENCE_LENGTH, BLOCK):
        stop = start + BLOCK
        here = pl.ds(pl.multiple_of(base + start, BLOCK), BLOCK)
        for first in range(0, heads, GROUP):
            stacked = jnp.concatenate(
                [whole_ref[here, h * HEAD_SIZE : (h + 1) * HEAD_SIZE] for h in range(first, first + GROUP)]
            )
            soft = probabilities(keys[:stop], stacked, start).astype(BF)
            attended = jnp.dot(values_t[:, :stop], soft, preferred_element_type=F32).astype(BF)
            for n in range(GROUP):
                h = first + n
                o_ref[h * HEAD_SIZE : (h + 1) * HEAD_SIZE, start:stop] = attended[:, n * BLOCK : (n + 1) * BLOCK]


def attended_transposed(place, parts, keys, values, turn, count, earlier=()):
    flat = [x for part in parts for x in part]
    rows, width = flat[0].shape
    tokens = keys.shape[0]
    kv = keys.shape[1] // HEAD_SIZE
    each = width // kv
    L = SEQUENCE_LENGTH
    small = pl.BlockSpec((L, HEAD_SIZE), lambda g, s, place: (place[PLACE_TURN + turn + s], g))
    spec = pltpu.PrefetchScalarGridSpec(
        num_scalar_prefetch=1,
        grid=(kv, count),
        in_specs=[pl.BlockSpec((rows, each), lambda g, s, place: (0, g))] * len(flat)
        + [small, small]
        + [pl.BlockSpec(memory_space=pl.ANY)] * len(earlier),
        out_specs=pl.BlockSpec((each, L), lambda g, s, place: (g, place[PLACE_TURN + turn + s])),
        scratch_shapes=[pltpu.VMEM((4 * rows, each), BF)],
    )
    return pl.pallas_call(
        functools.partial(forward_kernel, [len(part) for part in parts], turn, len(earlier)),
        grid_spec=spec,
        out_shape=jax.ShapeDtypeStruct((width, tokens), BF),
        input_output_aliases={3 + len(flat): 0} if earlier else {},
        compiler_params=SMALL,
        name="attention_forward",
        cost_estimate=COST,
    )(place, *flat, keys, values, *earlier)


def backward_kernel(slot, heads, groups, counts, place_ref, k_ref, v_ref, *rest):
    parts, rest = rest[: sum(counts)], rest[sum(counts) :]
    pieces, rest = rest[: sum(groups)], rest[sum(groups) :]
    if slot == 0:
        dq_ref, dk_ref, dv_ref, grad_ref, q_ref = rest
    else:
        _, dk_in, dv_in, dq_ref, dk_ref, dv_ref, grad_ref, q_ref = rest
    s = pl.program_id(0)
    L = SEQUENCE_LENGTH
    rows = grad_ref.shape[0] // 4

    def put(ref, chunk):
        for j in range(2):
            offset = pl.multiple_of(place_ref[PLACE_BLOCK + 2 * chunk + j], 64)
            grad_ref[pl.ds(offset, rows), :] = ref[j * rows : (j + 1) * rows, :]

    @pl.when(s == 0)
    def _():
        assemble(place_ref, parts, counts, q_ref)
        at = 0
        for chunk, count in enumerate(groups):
            if count == 1:
                put(pieces[at], chunk)
            else:
                for choice in range(2):
                    pl.when(place_ref[PLACE_END] == 1 - choice)(functools.partial(put, pieces[at + choice], chunk))
            at += count

    keys = k_ref[...]
    values = v_ref[...]
    keys_t = keys.T
    dk_ref[...] = dk_in[...] if slot % 2 else jnp.zeros((L, HEAD_SIZE), F32)
    dv_ref[...] = dv_in[...] if slot % 2 else jnp.zeros((L, HEAD_SIZE), F32)
    for start in range(0, L, BLOCK):
        stop = start + BLOCK
        here = pl.ds(pl.multiple_of(s * L + start, BLOCK), BLOCK)
        for first in range(0, heads, PAIR):
            stacked = stack(q_ref, here, first, first + PAIR)
            grads = stack(grad_ref, here, first, first + PAIR)
            soft = probabilities(keys[:stop], stacked, start)
            soft_grad = lax.dot_general(values[:stop], grads, CONTRACT_LAST, preferred_element_type=F32)
            dots = jnp.sum(soft * soft_grad, axis=0, keepdims=True)
            score_grad = (soft * (soft_grad - dots)).astype(BF)
            dv_ref[:stop, :] += jnp.dot(soft.astype(BF), grads, preferred_element_type=F32)
            dk_ref[:stop, :] += jnp.dot(score_grad, stacked, preferred_element_type=F32) * SCALE
            dq_t = (jnp.dot(keys_t[:, :stop], score_grad, preferred_element_type=F32) * SCALE).astype(BF)
            for n in range(PAIR):
                h = first + n
                dq_ref[start:stop, h * HEAD_SIZE : (h + 1) * HEAD_SIZE] = dq_t[:, n * BLOCK : (n + 1) * BLOCK].T


def attention_backward(slot, place, parts, keys, values, chunks, earlier):
    flat = [x for part in parts for x in part]
    pieces = [piece for chunk in chunks for piece in chunk]
    rows, width = flat[0].shape
    tokens = keys.shape[0]
    quarter = pieces[0].shape[1]
    L = SEQUENCE_LENGTH
    small = pl.BlockSpec((L, HEAD_SIZE), lambda s, place: (s, place[PLACE_KEY + slot]))
    wide = pl.BlockSpec((L, quarter), lambda s, place: (s, place[PLACE_HEAD + slot]))
    n = len(pieces) + len(flat)
    spec = pltpu.PrefetchScalarGridSpec(
        num_scalar_prefetch=1,
        grid=(tokens // L,),
        in_specs=[small, small]
        + [pl.BlockSpec((rows, quarter), lambda s, place: (0, place[PLACE_HEAD + slot]))] * len(flat)
        + [pl.BlockSpec(x.shape, lambda s, place: (0, 0)) for x in pieces]
        + ([] if slot == 0 else [pl.BlockSpec(memory_space=pl.ANY), small, small]),
        out_specs=[wide, small, small],
        scratch_shapes=[pltpu.VMEM((tokens, quarter), BF)] * 2,
    )
    sums = jax.ShapeDtypeStruct(keys.shape, F32)
    return pl.pallas_call(
        functools.partial(
            backward_kernel,
            slot,
            quarter // HEAD_SIZE,
            [len(chunk) for chunk in chunks],
            [len(part) for part in parts],
        ),
        grid_spec=spec,
        out_shape=[jax.ShapeDtypeStruct((tokens, width), BF), sums, sums],
        input_output_aliases={} if slot == 0 else {3 + n: 0, 4 + n: 1, 5 + n: 2},
        compiler_params=SMALL,
        name="attention_backward",
        cost_estimate=COST,
    )(place, keys, values, *flat, *pieces, *([] if slot == 0 else earlier))


def partial_kernel(place_ref, first_ref, second_ref, weight_ref, far_ref, near_ref, own_ref, both_ref):
    step = pl.program_id(0)
    rows = first_ref.shape[0]

    @pl.when(step == 0)
    def _():
        both_ref[:rows, :] = first_ref[...]
        both_ref[rows:, :] = second_ref[...]

    product = lax.dot_general(both_ref[...], weight_ref[...], CONTRACT_LAST, preferred_element_type=F32).astype(BF)
    for slot, (out_ref, at) in enumerate(((far_ref, 0), (near_ref, 0), (near_ref, 2 * rows), (own_ref, 0))):
        @pl.when(step == slot)
        def _(out_ref=out_ref, at=at):
            out_ref[at : at + 2 * rows, :] = product


def partial_products(place, first, second, weight):
    rows, features = first.shape
    quarter = weight.shape[0] // 4
    shapes = [(2 * rows, quarter), (4 * rows, quarter), (2 * rows, quarter)]
    same = lambda shape: pl.BlockSpec(shape, lambda k, place: (0, 0))
    spec = pltpu.PrefetchScalarGridSpec(
        num_scalar_prefetch=1,
        grid=(4,),
        in_specs=[
            same(first.shape),
            same(second.shape),
            pl.BlockSpec((quarter, features), lambda k, place: (place[PLACE_SEND + k], 0)),
        ],
        out_specs=[same(shape) for shape in shapes],
        scratch_shapes=[pltpu.VMEM((2 * rows, features), BF)],
    )
    return pl.pallas_call(
        partial_kernel,
        grid_spec=spec,
        out_shape=[jax.ShapeDtypeStruct(shape, BF) for shape in shapes],
        compiler_params=STREAMED,
        name="gradient_partial",
        cost_estimate=COST,
    )(place, first, second, weight)


def output_kernel(attended_ref, upstream_ref, out_ref):
    out_ref[...] = jnp.dot(attended_ref[...], upstream_ref[...], preferred_element_type=F32).astype(BF)


def output_gradient(attended, upstream, block=512):
    width, tokens = attended.shape
    features = upstream.shape[1]
    return pl.pallas_call(
        output_kernel,
        grid=(width // block,),
        in_specs=[pl.BlockSpec((block, tokens), lambda i: (i, 0)), pl.BlockSpec((tokens, features), lambda i: (0, 0))],
        out_specs=pl.BlockSpec((block, features), lambda i: (i, 0)),
        out_shape=jax.ShapeDtypeStruct((width, features), BF),
        compiler_params=PARAMS,
        name="output_gradient",
        cost_estimate=COST,
    )(attended, upstream)


def weights_kernel(n_ref, dq_ref, dk_ref, dv_ref, gq_ref, gk_ref, gv_ref):
    nt = n_ref[...].T
    gq_ref[...] = jnp.dot(nt, dq_ref[...], preferred_element_type=F32).astype(BF)
    gk_ref[...] = jnp.dot(nt, dk_ref[...].astype(BF), preferred_element_type=F32).astype(BF)
    gv_ref[...] = jnp.dot(nt, dv_ref[...].astype(BF), preferred_element_type=F32).astype(BF)

def weight_gradients(normed, dq, dk, dv, block=256):
    tokens, feats = normed.shape
    whole = lambda x: pl.BlockSpec(x.shape, lambda i:(0,0))
    out = lambda x: pl.BlockSpec((block,x.shape[1]), lambda i:(i,0))
    return pl.pallas_call(
        weights_kernel, grid=(feats//block,),
        in_specs=[pl.BlockSpec((tokens,block),lambda i:(0,i)),whole(dq),whole(dk),whole(dv)],
        out_specs=[out(dq),out(dk),out(dv)],
        out_shape=[jax.ShapeDtypeStruct((feats,x.shape[1]),BF) for x in (dq,dk,dv)],
        compiler_params=STREAMED, name="weight_gradients",
        cost_estimate=COST,
    )(normed,dq,dk,dv)

def input_kernel(half, place_ref, dq_ref, dk_ref, dv_ref, wq_ref, wk_ref, wv_ref, first_ref, second_ref, total_ref):
    rows = first_ref.shape[0]
    here = pl.ds(pl.multiple_of(place_ref[PLACE_HALF + half], 2 * rows), 2 * rows)
    total = lax.dot_general(dq_ref[here, :], wq_ref[...], CONTRACT_LAST, preferred_element_type=F32)
    total += lax.dot_general(dk_ref[here, :].astype(BF), wk_ref[...], CONTRACT_LAST, preferred_element_type=F32)
    total += lax.dot_general(dv_ref[here, :].astype(BF), wv_ref[...], CONTRACT_LAST, preferred_element_type=F32)
    total_ref[...] = total.astype(BF)
    first_ref[...] = total_ref[pl.ds(pl.multiple_of(place_ref[PLACE_SUB], rows), rows), :]
    second_ref[...] = total_ref[pl.ds(pl.multiple_of(place_ref[PLACE_SUB + 1], rows), rows), :]


def input_gradients(half, place, rows, dq, dk, dv, query_weight, key_matrix, value_matrix, block=512):
    features, width = query_weight.shape
    small = key_matrix.shape[1]
    whole = lambda x: pl.BlockSpec(x.shape, lambda i, place: (0, 0))
    strip = lambda x: pl.BlockSpec((block, x.shape[1]), lambda i, place: (i, 0))
    spec = pltpu.PrefetchScalarGridSpec(
        num_scalar_prefetch=1,
        grid=(features // block,),
        in_specs=[whole(dq), whole(dk), whole(dv), strip(query_weight), strip(key_matrix), strip(value_matrix)],
        out_specs=[pl.BlockSpec((rows, block), lambda i, place: (0, i))] * 2,
        scratch_shapes=[pltpu.VMEM((2 * rows, block), BF)],
    )
    return pl.pallas_call(
        functools.partial(input_kernel, half),
        grid_spec=spec,
        out_shape=[jax.ShapeDtypeStruct((rows, features), BF)] * 2,
        compiler_params=PARAMS,
        name="input_gradients",
        cost_estimate=COST,
    )(place, dq, dk, dv, query_weight, key_matrix, value_matrix)

def attend(query_token_rows, key_token_rows, value_token_rows, gradient_rows):
    token_count = query_token_rows.shape[0]
    kv_groups = key_token_rows.shape[1] // HEAD_SIZE
    group_width = QUERY_HEADS // KEY_VALUE_HEADS
    score_scale = HEAD_SIZE ** (-0.5)
    query_head_rows = query_token_rows.reshape(token_count, kv_groups, group_width, HEAD_SIZE)
    gradient_heads = gradient_rows.reshape(token_count, kv_groups, group_width, HEAD_SIZE)
    key_head_rows = key_token_rows.reshape(token_count, kv_groups, HEAD_SIZE)
    value_head_rows = value_token_rows.reshape(token_count, kv_groups, HEAD_SIZE)
    scores = (
        jnp.einsum(
            "qagd,kad->agqk", query_head_rows, key_head_rows, preferred_element_type=jnp.float32
        )
        * score_scale
    )
    positions = jnp.arange(token_count, dtype=jnp.int32)
    allowed = positions[None, :] <= positions[:, None]
    scores = jnp.where(allowed, scores, -jnp.inf)
    top_score = jnp.max(scores, axis=-1, keepdims=True)
    raised = jnp.exp(scores - top_score)
    softmax = raised / jnp.sum(raised, axis=-1, keepdims=True)
    soft_bf = softmax.astype(jnp.bfloat16)
    attended = jnp.einsum(
        "agqk,kad->qagd", soft_bf, value_head_rows, preferred_element_type=jnp.float32
    )
    attended = attended.astype(jnp.bfloat16).reshape(token_count, -1)
    soft_grad = jnp.einsum(
        "qagd,kad->agqk", gradient_heads, value_head_rows, preferred_element_type=jnp.float32
    )
    row_dots = jnp.sum(softmax * soft_grad, axis=-1, keepdims=True)
    score_grad = (softmax * (soft_grad - row_dots)).astype(jnp.bfloat16)
    query_grad = (
        jnp.einsum("agqk,kad->qagd", score_grad, key_head_rows, preferred_element_type=jnp.float32)
        * score_scale
    )
    query_grad = query_grad.astype(jnp.bfloat16).reshape(token_count, -1)
    key_gradient = (
        jnp.einsum(
            "agqk,qagd->kad", score_grad, query_head_rows, preferred_element_type=jnp.float32
        )
        * score_scale
    )
    value_gradient = jnp.einsum(
        "agqk,qagd->kad", soft_bf, gradient_heads, preferred_element_type=jnp.float32
    )
    return (
        attended,
        query_grad,
        key_gradient.reshape(token_count, -1),
        value_gradient.reshape(token_count, -1),
    )


def general_shards(
    normed,
    queries,
    stored_keys,
    stored_values,
    upstream,
    query_weight,
    key_matrix,
    value_matrix,
    output_weight,
):
    tokens = stored_keys.shape[0]
    normed_all, upstream_all = (
        lax.all_gather(normed, ("col", "sub"), axis=0, tiled=True),
        lax.all_gather(upstream, ("col", "sub"), axis=0, tiled=True),
    )
    contract_last = (((1,), (1,)), ((), ()))
    contract_first = (((0,), (0,)), ((), ()))
    partial_sum = lax.dot_general(
        upstream_all, output_weight, contract_last, preferred_element_type=jnp.float32
    )
    attended_gradient = lax.psum(partial_sum.astype(jnp.bfloat16), "row")
    query_token_rows = lax.all_gather(queries, "row", axis=0, tiled=True)
    sequence_list = tokens // SEQUENCE_LENGTH

    def per_sequence(blocks):
        return attend(blocks[0], blocks[1], blocks[2], blocks[3])

    result_list = lax.map(
        per_sequence,
        (
            query_token_rows.reshape(sequence_list, SEQUENCE_LENGTH, -1),
            stored_keys.reshape(sequence_list, SEQUENCE_LENGTH, -1),
            stored_values.reshape(sequence_list, SEQUENCE_LENGTH, -1),
            attended_gradient.reshape(sequence_list, SEQUENCE_LENGTH, -1),
        ),
    )
    attended_all = result_list[0].reshape(tokens, -1)
    query_all = result_list[1].reshape(tokens, -1)
    key_all = result_list[2].reshape(tokens, -1).astype(jnp.bfloat16)
    value_all = result_list[3].reshape(tokens, -1).astype(jnp.bfloat16)
    grad_output = lax.dot_general(
        attended_all, upstream_all, contract_first, preferred_element_type=jnp.float32
    ).astype(jnp.bfloat16)
    grad_query = lax.dot_general(
        normed_all, query_all, contract_first, preferred_element_type=jnp.float32
    ).astype(jnp.bfloat16)
    grad_key = lax.dot_general(
        normed_all, key_all, contract_first, preferred_element_type=jnp.float32
    ).astype(jnp.bfloat16)
    grad_value = lax.dot_general(
        normed_all, value_all, contract_first, preferred_element_type=jnp.float32
    ).astype(jnp.bfloat16)
    summed = lax.dot_general(
        query_all, query_weight, contract_last, preferred_element_type=jnp.float32
    )
    summed = summed + lax.dot_general(
        key_all, key_matrix, contract_last, preferred_element_type=jnp.float32
    )
    grad_normed = lax.psum_scatter(
        (
            summed
            + lax.dot_general(
                value_all, value_matrix, contract_last, preferred_element_type=jnp.float32
            )
        ).astype(jnp.bfloat16),
        ("col", "sub"),
        scatter_dimension=0,
        tiled=True,
    )
    return (grad_normed, grad_query, grad_key, grad_value, grad_output)


def swap(x, axis):
    return lax.ppermute(x, axis, [(0, 1), (1, 0)])


def inward(x):
    return lax.ppermute(x, "row", [(0, 1), (3, 2)])


def across(x):
    return lax.ppermute(x, "row", [(1, 2), (2, 1)])


def outward(x):
    return lax.ppermute(x, "row", [(1, 0), (2, 3)])


def paired(x):
    return lax.ppermute(x, "row", [(0, 1), (1, 0), (2, 3), (3, 2)])


def after(value, others):
    return lax.optimization_barrier((value, others))


def plus(*terms):
    return sum(term.astype(F32) for term in terms).astype(BF)


def shards(
    normed,
    queries,
    stored_keys,
    stored_values,
    upstream,
    query_weight,
    key_matrix,
    value_matrix,
    output_weight,
):
    row = lax.axis_index("row")
    col = lax.axis_index("col")
    sub = lax.axis_index("sub")
    here = 2 * col + sub
    rows = upstream.shape[0]
    half = 2 * rows
    is_end = (row == 0) | (row == 3)
    index = jnp.arange(PLACE_TURN + 3, dtype=jnp.int32)
    table = jnp.array(
        [
            SEND_ORDER[r]
            + HEAD_ORDER[r]
            + tuple(q // 2 for q in HEAD_ORDER[r])
            + (0,) * 9
            + tuple(rows * q for q in HEAD_ORDER[r])
            + TURN_ORDER[r]
            for r in range(4)
        ]
    )
    place = jnp.sum(jnp.where(jnp.arange(4)[:, None] == row, table, 0), axis=0).astype(jnp.int32)
    for at, value in enumerate(
        [rows * (here ^ j) for j in range(4)]
        + [half * (1 - col), half * col, rows * (1 - sub), rows * sub, is_end.astype(jnp.int32)]
    ):
        place = jnp.where(index == PLACE_BLOCK + at, value.astype(jnp.int32), place)

    def backward(slot, pieces, results):
        return attention_backward(slot, place, query_parts, stored_keys, stored_values, pieces, results)

    first_up = swap(upstream, "sub")
    query_pair = paired(queries)
    second_up = swap(upstream, "col")
    query_mid = across(queries)
    a_far, a_near, a_own = partial_products(place, upstream, first_up, output_weight)
    (query_pair, query_mid), a_far = after((query_pair, query_mid), a_far)
    query_far = across(query_pair)
    query_out = outward(query_mid)
    (second_up, normed, late_upstream, a_far, a_near), (query_pair, query_mid) = after(
        (second_up, normed, upstream, a_far, a_near), (query_pair, query_mid)
    )
    a_in0 = inward(a_far)
    a_in = inward(a_near)
    third_up = swap(second_up, "sub")
    upstream_all = lax.all_gather(late_upstream, ("col", "sub"), axis=0, tiled=True)
    normed_all = lax.all_gather(normed, ("col", "sub"), axis=0, tiled=True)
    b_far, b_near, b_own = partial_products(place, second_up, third_up, output_weight)
    b_in0 = inward(b_far)
    a_in0, b_far = after(a_in0, b_far)
    a_mid0 = across(plus(a_far, a_in0))
    query_far, a_in0 = after(query_far, a_in0)
    query_last = outward(query_far)

    (a_mid0, query_out), query_far = after((a_mid0, query_out), query_far)
    a_out = outward(plus(a_near[half:], a_mid0))
    a_in, query_far = after(a_in, query_far)
    a_mid1 = across(plus(a_near[:half], a_in[:half]))
    b_in0, a_in = after(b_in0, a_in)
    b_mid0 = across(plus(b_far, b_in0))
    b_in = inward(b_near)
    query_out, b_in0 = after(query_out, b_in0)
    some_parts = [(queries,), (query_pair,), (query_out, query_mid)]
    attended = attended_transposed(place, some_parts, stored_keys, stored_values, 0, 2)

    (a_out, a_mid1), attended = after((a_out, a_mid1), attended)
    own_a = plus(a_own, a_in[half:], a_mid1, a_out)
    pair_a = paired(own_a)
    mid_a = across(own_a)
    b_mid0, own_a = after(b_mid0, own_a)
    b_out = outward(plus(b_near[half:], b_mid0))
    b_in, b_mid0 = after(b_in, b_mid0)
    b_mid1 = across(plus(b_near[:half], b_in[:half]))

    query_parts = some_parts + [(query_last, query_far)]
    attended = attended_transposed(place, query_parts, stored_keys, stored_values, 2, 1, [attended])
    (pair_a, mid_a), attended = after((pair_a, mid_a), attended)
    far_a = across(pair_a)
    out_a = outward(mid_a)
    (attended, upstream_all), (pair_a, mid_a) = after((attended, upstream_all), (pair_a, mid_a))
    grad_output = output_gradient(attended, upstream_all)
    (b_out, b_mid1), grad_output = after((b_out, b_mid1), grad_output)
    own_b = plus(b_own, b_in[half:], b_mid1, b_out)
    pair_b = paired(own_b)
    mid_b = across(own_b)
    results = backward(0, [(own_a,), (own_b,)], None)
    (far_a, out_a), results = after((far_a, out_a), results)
    last_a = outward(far_a)

    pair_b, mid_b, results = lax.optimization_barrier((pair_b, mid_b, results))
    far_b = across(pair_b)
    out_b = outward(mid_b)
    results = backward(1, [(pair_a,), (pair_b,)], results)

    far_b, out_b, results = lax.optimization_barrier((far_b, out_b, results))
    last_b = outward(far_b)
    results = backward(2, [(out_a, mid_a), (out_b, mid_b)], results)
    (last_a, last_b), results = after((last_a, last_b), results)
    query_grad, key_grad, value_grad = backward(3, [(last_a, far_a), (last_b, far_b)], results)

    weights = (query_grad, key_grad, value_grad, query_weight, key_matrix, value_matrix)
    to_sub, to_col = input_gradients(0, place, rows, *weights)
    to_col = to_col + swap(to_sub, "sub")
    from_col = swap(to_col, "col")
    weights, to_col = after(weights, to_col)
    to_sub, kept = input_gradients(1, place, rows, *weights)
    from_sub = swap(to_sub, "sub")
    normed_all, kept = after(normed_all, kept)
    grad_query, grad_key, grad_value = weight_gradients(normed_all, query_grad, key_grad, value_grad, block=512)
    from_col, _ = after(from_col, grad_query)
    from_sub, from_col = after(from_sub, from_col)
    grad_normed = plus(kept, from_sub, from_col)
    return (grad_normed, grad_query, grad_key, grad_value, grad_output)


def solution(mesh):
    in_specs = (
        P(("groups", "col", "sub"), "row"),
        P(("groups", "row"), ("col", "sub")),
        P("groups", ("col", "sub")),
        P("groups", ("col", "sub")),
        P(("groups", "col", "sub"), "row"),
        P(("groups", "row"), ("col", "sub")),
        P(("groups", "row"), ("col", "sub")),
        P(("groups", "row"), ("col", "sub")),
        P(("groups", "col", "sub"), "row"),
    )
    out_specs = (
        P(("groups", "col", "sub"), "row"),
        P(("groups", "row"), ("col", "sub")),
        P(("groups", "row"), ("col", "sub")),
        P(("groups", "row"), ("col", "sub")),
        P(("groups", "col", "sub"), "row"),
    )
    small = tuple(mesh.shape[axis] for axis in ("row", "col", "sub")) == (4, 2, 2)
    return jax.shard_map(shards if small else general_shards, mesh=mesh, in_specs=in_specs, out_specs=out_specs, check_vma=False)
```
